32 devices in a mesh: dp: 8 (over y, x, core), layer: 4 (over z).
Axes of the slice: x: 2, y: 2, z: 4, core: 2. Of those that a mesh axis runs over, the one named last changes fastest.
Arguments:
- coords: float32 [3, 4096], P(None, ('dp', 'layer')), may hold values from -4 to 4
- sample_ids: int32 [4096], P(('dp', 'layer')), may hold values from 0 to 262143
- pool: float32 [2097152], P('dp'), may hold values from -6 to 6
- in_weight: float32 [3, 1024], replicated, may hold values from -3.5 to 3.5
- in_bias: float32 [1024], replicated, may hold values from -1 to 1
- hidden: bfloat16 [2, 1024, 1024], replicated, may hold values from -0.1875 to 0.1875
- out_weight: float32 [1024, 4], replicated, may hold values from -0.1875 to 0.1875
Outputs:
- update: bfloat16 [2, 1024, 1024], replicated
- point_loss: float32 [4096], P(('dp', 'layer'))
The draws below stay inside these ranges and needn't reach their ends.
Inputs may be any that keep to these rules, and one draw needn't show every extreme that they name: sample_ids[p] is an offset into the pool block of 262144 entries held by dp index p // (128 * 4).
All inputs are finite; a program needn't handle non-finite values.
Results may differ from the reference program's by a relative error of at most 0.011.
Values may be sent and summed in bfloat16 or wider, within the bound.
A program may use at most 128 MiB of HBM per device.

```python
import jax
import jax.numpy as jnp
from jax import lax

W = 1024
PTS_DEV = 128
POOL_DEV = 262144
LAYERS = 2
BLK = 128
POINTS = 4096
POOL = 2097152
N_DP = 8
N_LAYER = 4


def plant(entries, rng, low, high):
    extent = entries.shape
    spot = [jax.random.randint(jax.random.fold_in(rng, axis), (), 0, extent[axis]) for axis in range(len(extent))]
    entries = entries.at[tuple(spot)].set(low)
    longest = extent.index(max(extent))
    spot[longest] = (spot[longest] + 1) % extent[longest]
    return entries.at[tuple(spot)].set(high)


def shard_levels(rng, shape, shards, least, high):
    factor_of, own = 1.0, jax.random.fold_in(rng, 6)
    for dim, shards_of in shards:
        heights = jnp.exp(jax.random.uniform(jax.random.fold_in(own, dim), (shards_of,), jnp.float32, least / len(shards), high / len(shards)))
        factor_of = factor_of * jnp.repeat(heights, shape[dim] // shards_of).reshape([-1 if axis == dim else 1 for axis in range(len(shape))])
    return factor_of


def normal_values(stream_key, shape, scale, limit, split=(), kind=jnp.bfloat16):
    entries = scale * jax.random.normal(stream_key, shape, jnp.float32)
    if split:
        entries = entries * shard_levels(stream_key, shape, split, -0.22, 0.18)
    return jnp.clip(entries, -limit, limit).astype(kind)


def setup_inputs(seed: int = 0) -> dict:
    arg_keys = jax.random.split(jax.random.key(seed), 8)
    return {
        "coords": normal_values(arg_keys[0], (3, POINTS), 1.0, 4.0, ((1, 32),), jnp.float32),
        "sample_ids": plant(jax.random.randint(arg_keys[1], (POINTS,), 0, POOL_DEV), jax.random.fold_in(arg_keys[1], 1), 0, POOL_DEV - 1).astype(jnp.int32),
        "pool": normal_values(arg_keys[2], (POOL,), 1.5, 6.0, ((0, 8),), jnp.float32),
        "in_weight": normal_values(arg_keys[3], (3, W), 3 ** -0.5, 3.5, (), jnp.float32),
        "in_bias": jnp.clip(jax.random.uniform(arg_keys[4], (W,), jnp.float32, -1.0, 1.0), -1.0, 1.0),
        "hidden": normal_values(arg_keys[5], (LAYERS, W, W), W ** -0.5, 0.1875),
        "out_weight": normal_values(arg_keys[6], (W, 4), W ** -0.5, 0.1875, (), jnp.float32),
    }


VISCOSITY = 0.1
DAMPING = 0.1

def taylor_tanh(pre, pre_grad, pre_lap):
    act = jnp.tanh(pre)
    slope = 1.0 - act * act
    act_lap = slope * pre_lap - 2.0 * act * slope * lax.optimization_barrier(jnp.sum(pre_grad * pre_grad, axis=0))
    return (act, slope * pre_grad, act_lap)

def network(nudges, coords, in_weight, in_bias, hidden, out_weight):
    count = coords.shape[1]
    width = in_weight.shape[1]
    pre = jnp.dot(coords.T, in_weight, precision=lax.Precision.HIGHEST) + in_bias
    pre_grad = jnp.broadcast_to(in_weight[:, None, :], (3, count, width))
    pre_lap = jnp.zeros((count, width), in_weight.dtype)
    stacks = []
    for level in range(hidden.shape[0]):
        act, act_grad, act_lap = taylor_tanh(pre, pre_grad, pre_lap)
        stack = jnp.concatenate([act[None], act_grad, act_lap[None]], 0).astype(jnp.bfloat16).reshape(5 * count, width)
        stacks.append(stack)
        mixed = jnp.dot(stack.astype(jnp.float32), hidden[level].astype(jnp.float32), preferred_element_type=jnp.float32) + nudges[level]
        mixed = mixed.reshape(5, count, width)
        pre, pre_grad, pre_lap = (mixed[0], mixed[1:4], mixed[4])
    act, act_grad, act_lap = taylor_tanh(pre, pre_grad, pre_lap)
    field = jnp.dot(act, out_weight, precision=lax.Precision.HIGHEST)
    field_grad = jnp.einsum('kpw,wc->kpc', act_grad, out_weight, precision=lax.Precision.HIGHEST)
    field_lap = jnp.dot(act_lap, out_weight, precision=lax.Precision.HIGHEST)
    return (field, field_grad, field_lap, stacks)

def residual_loss(field, field_grad, field_lap):
    velocity = field[:, :3].T
    advect = lax.optimization_barrier(jnp.sum(velocity[:, :, None] * field_grad[:, :, :3], axis=0))
    momentum = advect + field_grad[:, :, 3].T - VISCOSITY * field_lap[:, :3]
    continuity = field_grad[0, :, 0] + field_grad[1, :, 1] + field_grad[2, :, 2]
    return 0.5 * (lax.optimization_barrier(jnp.sum(momentum * momentum, axis=1)) + continuity * continuity)

def point_terms(coords, weight, in_weight, in_bias, hidden, out_weight, total):
    count = coords.shape[1]
    width = in_weight.shape[1]
    zeros = [jnp.zeros((5 * count, width), jnp.float32) for level in range(hidden.shape[0])]

    def loss_of(nudges):
        field, field_grad, field_lap, stacks = network(nudges, coords, in_weight, in_bias, hidden, out_weight)
        losses = residual_loss(field, field_grad, field_lap)
        return (jnp.sum(weight * losses) / total, (losses, stacks))
    value, pull, extra = jax.vjp(loss_of, zeros, has_aux=True)
    losses, stacks = extra
    deltas = [piece.astype(jnp.bfloat16) for piece in pull(jnp.ones_like(value))[0]]
    return (losses, stacks, deltas)

def damped_inverse(factor, scale):
    size = factor.shape[-1]
    eye = jnp.eye(size, dtype=jnp.float32)
    damped = factor + DAMPING * scale * eye
    lower = jnp.linalg.cholesky(damped)
    return jax.scipy.linalg.cho_solve((lower, True), jnp.broadcast_to(eye, damped.shape).astype(damped.dtype))

def reference(coords, sample_ids, pool, in_weight, in_bias, hidden, out_weight):
    owner = (jnp.arange(POINTS) // (PTS_DEV * N_LAYER)).astype(jnp.int32)
    weight = jax.nn.softplus(pool[owner * POOL_DEV + sample_ids.astype(jnp.int32)])
    group = PTS_DEV * N_DP
    blocks = POINTS // group
    coords_b = coords.reshape(3, blocks, group).transpose(1, 0, 2)
    weight_b = weight.reshape(blocks, group)
    init = (jnp.zeros((LAYERS, N_DP, BLK, BLK), jnp.float32), jnp.zeros((LAYERS, N_DP, BLK, BLK), jnp.float32), jnp.zeros((LAYERS, W, W), jnp.float32))

    def step(carry, item):
        coords_i, weight_i = item
        losses, stacks, deltas = point_terms(coords_i, weight_i, in_weight, in_bias, hidden, out_weight, POINTS)
        sum_a, sum_g, sum_grad = carry
        new_a, new_g, new_grad = ([], [], [])
        for level in range(LAYERS):
            rows_a = stacks[level].astype(jnp.float32).reshape(-1, N_DP, BLK)
            rows_g = deltas[level].astype(jnp.float32).reshape(-1, N_DP, BLK)
            new_a.append(jnp.einsum('rnb,rnc->nbc', rows_a, rows_a, precision=lax.Precision.HIGHEST))
            new_g.append(jnp.einsum('rnb,rnc->nbc', rows_g, rows_g, precision=lax.Precision.HIGHEST))
            new_grad.append(jnp.dot(stacks[level].T.astype(jnp.float32), deltas[level].astype(jnp.float32), preferred_element_type=jnp.float32))
        return ((sum_a + jnp.stack(new_a), sum_g + jnp.stack(new_g), sum_grad + jnp.stack(new_grad)), losses)
    (sum_a, sum_g, sum_grad), losses = lax.scan(step, init, (coords_b, weight_b))
    factor_a = sum_a / POINTS
    factor_g = sum_g * POINTS
    trace_a = lax.optimization_barrier(jnp.sum(jnp.trace(factor_a, axis1=2, axis2=3), axis=1)) / W
    trace_g = lax.optimization_barrier(jnp.sum(jnp.trace(factor_g, axis1=2, axis2=3), axis=1)) / W
    inv_a = damped_inverse(factor_a, trace_a[:, None, None, None])
    inv_g = damped_inverse(factor_g, trace_g[:, None, None, None])
    grad_blocks = sum_grad.reshape(LAYERS, N_DP, BLK, N_DP, BLK)
    left = jnp.einsum('lnab,lnbjc->lnajc', inv_a, grad_blocks, precision=lax.Precision.HIGHEST)
    both = jnp.einsum('lnajc,ljcq->lnajq', left, inv_g, precision=lax.Precision.HIGHEST)
    update = both.reshape(LAYERS, W, W).astype(jnp.bfloat16)
    return (update, losses.reshape(POINTS))
```

```python
import functools

import jax
import jax.numpy as jnp
from jax import lax
from jax.experimental import pallas as pl
from jax.experimental.pallas import tpu as pltpu
from jax.sharding import PartitionSpec as P

VISCOSITY = 0.1
DAMPING = 0.1


def taylor_tanh(pre, pre_grad, pre_lap):
    act = jnp.tanh(pre)
    slope = 1.0 - act * act
    act_lap = slope * pre_lap - 2.0 * act * slope * jnp.sum(pre_grad * pre_grad, axis=0)
    return (act, slope * pre_grad, act_lap)


def network(nudges, coords, in_weight, in_bias, hidden, out_weight):
    count = coords.shape[1]
    width = in_weight.shape[1]
    pre = jnp.dot(coords.T, in_weight, precision=lax.Precision.HIGHEST) + in_bias
    pre_grad = jnp.broadcast_to(in_weight[:, None, :], (3, count, width))
    pre_lap = jnp.zeros((count, width), in_weight.dtype)
    stacks = []
    for level in range(hidden.shape[0]):
        act, act_grad, act_lap = taylor_tanh(pre, pre_grad, pre_lap)
        stack = (
            jnp.concatenate([act[None], act_grad, act_lap[None]], 0)
            .astype(jnp.bfloat16)
            .reshape(5 * count, width)
        )
        stacks.append(stack)
        mixed = jnp.dot(stack, hidden[level], preferred_element_type=jnp.float32) + nudges[level]
        mixed = mixed.reshape(5, count, width)
        pre, pre_grad, pre_lap = (mixed[0], mixed[1:4], mixed[4])
    act, act_grad, act_lap = taylor_tanh(pre, pre_grad, pre_lap)
    field = jnp.dot(act, out_weight, precision=lax.Precision.HIGHEST)
    field_grad = jnp.einsum("kpw,wc->kpc", act_grad, out_weight, precision=lax.Precision.HIGHEST)
    field_lap = jnp.dot(act_lap, out_weight, precision=lax.Precision.HIGHEST)
    return (field, field_grad, field_lap, stacks)


def residual_loss(field, field_grad, field_lap):
    velocity = field[:, :3].T
    advect = jnp.sum(velocity[:, :, None] * field_grad[:, :, :3], axis=0)
    momentum = advect + field_grad[:, :, 3].T - VISCOSITY * field_lap[:, :3]
    continuity = field_grad[0, :, 0] + field_grad[1, :, 1] + field_grad[2, :, 2]
    return 0.5 * (jnp.sum(momentum * momentum, axis=1) + continuity * continuity)


def point_terms(coords, weight, in_weight, in_bias, hidden, out_weight, total):
    count = coords.shape[1]
    width = in_weight.shape[1]
    zeros = [jnp.zeros((5 * count, width), jnp.float32) for level in range(hidden.shape[0])]

    def loss_of(nudges):
        field, field_grad, field_lap, stacks = network(
            nudges, coords, in_weight, in_bias, hidden, out_weight
        )
        losses = residual_loss(field, field_grad, field_lap)
        return (jnp.sum(weight * losses) / total, (losses, stacks))

    value, pull, extra = jax.vjp(loss_of, zeros, has_aux=True)
    losses, stacks = extra
    deltas = [piece.astype(jnp.bfloat16) for piece in pull(jnp.ones_like(value))[0]]
    return (losses, stacks, deltas)


def damped_inverse(factor, scale):
    size = factor.shape[-1]
    eye = jnp.eye(size, dtype=jnp.float32)
    damped = factor + DAMPING * scale * eye
    lower = jnp.linalg.cholesky(damped)
    return jax.scipy.linalg.cho_solve((lower, True), jnp.broadcast_to(eye, damped.shape))


MESH = pl.DeviceIdType.MESH
TN = (((0,), (0,)), ((), ()))


def mm(a, b, dims):
    return lax.dot_general(a, b, dims, preferred_element_type=jnp.float32)


def high(a, b):
    return jnp.dot(a, b, precision=lax.Precision.HIGHEST, preferred_element_type=jnp.float32)


def invert(damped):
    size = damped.shape[0]
    row_id = lax.broadcasted_iota(jnp.int32, (size, size), 0)
    col_id = lax.broadcasted_iota(jnp.int32, (size, size), 1)

    def step(k, a):
        in_row = row_id == k
        in_col = col_id == k
        row = jnp.sum(jnp.where(in_row, a, 0.0), axis=0, keepdims=True)
        col = jnp.sum(jnp.where(in_col, a, 0.0), axis=1, keepdims=True)
        pivot = jnp.sum(jnp.where(in_col[:1], row, 0.0), axis=1, keepdims=True)
        row = jnp.where(in_col[:1], 1.0, row) * (1.0 / pivot)
        col = jnp.where(in_row[:, :1], -1.0, col)
        return jnp.where(in_row | in_col, 0.0, a) - col * row

    return lax.fori_loop(0, size, step, damped)


def exchange_kernel(
    n_dp, n_layer, total, *refs
):
    levels = n_layer // 2
    n_chip = n_dp // 2
    stacks, deltas = refs[:levels], refs[levels : 2 * levels]
    (out, f_send, f_own, fc_recv, fp_recv, fz_send, fz_recv, tr_send, tr_recv, inv_own, inv_a, inv_g,
     g_send, g_own, gc_recv, gp_recv, gz_send, gz_recv,
     s_fc, r_fc, s_fp, r_fp, s_fz, r_fz, s_tr, r_tr, s_ia, r_ia, s_ig, r_ig,
     s_gc, r_gc, s_gp, r_gp, s_gz, r_gz, s_uz, s_up, s_uc, r_u) = refs[2 * levels :]
    width = stacks[0].shape[1]
    block = width // n_dp
    half = width // 2
    n_half = n_dp // 2
    d = lax.axis_index("dp")
    l = lax.axis_index("layer")
    chip, core = d // 2, d % 2
    level, kind = l // 2, l % 2
    sib = (chip * 2 + 1 - core, l)

    def remote(src, dst, send, recv, dev):
        return pltpu.make_async_remote_copy(
            src_ref=src, dst_ref=dst, send_sem=send, recv_sem=recv, device_id=dev, device_id_type=MESH
        )

    def other(k):
        return lax.rem(chip + 1 + k, n_chip)

    def loop(n, body):
        def run(i, carry):
            body(i)
            return carry

        lax.fori_loop(0, n, run, 0)

    barrier = pltpu.get_barrier_semaphore()

    def greet(k):
        to = lax.rem(d + 1 + k, n_dp)
        pl.semaphore_signal(barrier, inc=1, device_id=(to, l), device_id_type=MESH)

    def greet_mate(k):
        pl.semaphore_signal(barrier, inc=1, device_id=(k, 2 * level + 1 - kind), device_id_type=MESH)

    def greet_layer(k):
        to = lax.rem(2 * level + 2 + k, n_layer)
        pl.semaphore_signal(barrier, inc=1, device_id=(d, to), device_id_type=MESH)

    loop(n_dp - 1, greet)
    loop(n_dp, greet_mate)
    loop(n_layer - 2, greet_layer)

    def columns(ref, dp):
        return ref[:, pl.ds(pl.multiple_of(dp * block, block), block)]

    def factor(lay, dp):
        rows = columns(stacks[lay // 2] if lay % 2 == 0 else deltas[lay // 2], dp)
        term = mm(rows, rows, TN)
        return term / total if lay % 2 == 0 else term * total

    def grad(lay, dp):
        cols = slice((lay % 2) * half, (lay % 2 + 1) * half)
        return mm(columns(stacks[lay // 2], dp), deltas[lay // 2][:, cols], TN)

    def fc_copy(c):
        return remote(f_send.at[c], fc_recv.at[c], s_fc.at[c], r_fc.at[c], sib)

    def gc_copy(c):
        return remote(g_send.at[c], gc_recv.at[c], s_gc.at[c], r_gc.at[c], sib)

    def fp_copy(c, slot):
        return remote(f_own.at[c], fp_recv.at[slot], s_fp.at[c], r_fp.at[slot], (2 * c + core, l))

    def gp_copy(c, lay, slot):
        return remote(
            g_own.at[c, lay], gp_recv.at[slot, lay], s_gp.at[c, lay], r_gp.at[slot, lay], (2 * c + core, l)
        )

    def fz_copy(lay, slot):
        return remote(fz_send.at[lay], fz_recv.at[slot], s_fz.at[lay], r_fz.at[slot], (d, lay))

    def gz_copy(lay, slot):
        return remote(gz_send.at[lay], gz_recv.at[slot], s_gz.at[lay], r_gz.at[slot], (d, lay))

    def first_factor(k):
        c = other(k)
        for lay in range(n_layer):
            f_send[c, lay] = factor(lay, 2 * c + 1 - core)

    loop(n_chip, first_factor)
    pl.semaphore_wait(barrier, 2 * n_dp - 1 + n_layer - 2)
    loop(n_chip, lambda k: fc_copy(other(k)).start())

    def first_grad(k):
        c = other(k)
        for lay in range(n_layer):
            g_send[c, lay] = grad(lay, 2 * c + 1 - core)
        gc_copy(c).start()

    loop(n_chip, first_grad)

    def second_factor(k):
        c = other(k)
        fc_copy(c).wait_recv()
        for lay in range(n_layer):
            f_own[c, lay] = factor(lay, 2 * c + core) + fc_recv[c, lay]

    def send_factor(k):
        second_factor(k)
        fp_copy(other(k), chip).start()

    loop(n_chip - 1, send_factor)
    second_factor(n_chip - 1)

    def second_grad(k):
        c = other(k)
        gc_copy(c).wait_recv()
        for lay in range(n_layer):
            g_own[c, lay] = grad(lay, 2 * c + core) + gc_recv[c, lay]

    def send_grad(k):
        second_grad(k)
        loop(n_layer, lambda lay: gp_copy(other(k), lay, chip).start())

    loop(n_chip - 1, send_grad)
    second_grad(n_chip - 1)

    loop(n_chip - 1, lambda k: fp_copy(other(k), other(k)).wait_recv())

    def plane_factor(lay):
        value = f_own[chip, lay]
        for k in range(n_chip - 1):
            value = value + fp_recv[other(k), lay]
        fz_send[lay] = value

    def send_plane_factor(k):
        lay = lax.rem(l + 1 + k, n_layer)
        plane_factor(lay)
        fz_copy(lay, l).start()

    loop(n_layer - 1, send_plane_factor)
    plane_factor(l)
    mine = fz_send[l]
    for k in range(n_layer - 1):
        lay = lax.rem(l + 1 + k, n_layer)
        fz_copy(lay, lay).wait_recv()
        mine = mine + fz_recv[lay]

    diagonal = lax.broadcasted_iota(jnp.int32, (block, block), 0) == lax.broadcasted_iota(
        jnp.int32, (block, block), 1
    )
    trace = jnp.sum(jnp.sum(jnp.where(diagonal, mine, 0.0), axis=0, keepdims=True), axis=1, keepdims=True)
    tr_send[...] = jnp.broadcast_to(trace, tr_send.shape)

    def tr_copy(to, slot):
        return remote(tr_send, tr_recv.at[slot], s_tr.at[to], r_tr.at[slot], (to, l))

    loop(n_dp - 1, lambda k: tr_copy(lax.rem(d + 1 + k, n_dp), d).start())
    traces = tr_send[...]
    for k in range(n_dp - 1):
        to = lax.rem(d + 1 + k, n_dp)
        tr_copy(to, to).wait_recv()
        traces = traces + tr_recv[to]
    damped = mine + jnp.where(diagonal, DAMPING / width * traces[:1], 0.0)
    inv_own[...] = invert(damped)

    def ia_copy():
        return remote(inv_own, inv_a, s_ia, r_ia, (d, 2 * level + 1))

    def ig_copy(to, lay, slot):
        return remote(inv_own, inv_g.at[slot], s_ig.at[to], r_ig.at[slot], (to, lay))

    user = 2 * level + d // n_half

    @pl.when(kind == 0)
    def _():
        ia_copy().start()
        inv_a[...] = inv_own[...]

    @pl.when(kind == 1)
    def _():
        loop(n_dp - 1, lambda k: ig_copy(lax.rem(d + 1 + k, n_dp), user, d % n_half).start())

        @pl.when(user == l)
        def _():
            inv_g[d % n_half] = inv_own[...]

        @pl.when(user != l)
        def _():
            ig_copy(d, user, d % n_half).start()

    def plane_grad(lay):
        value = g_own[chip, lay]
        for k in range(n_chip - 1):
            gp_copy(other(k), lay, other(k)).wait_recv()
            value = value + gp_recv[other(k), lay]
        gz_send[lay] = value

    def send_plane_grad(lay):
        plane_grad(lay)

        @pl.when(lay != l)
        def _():
            gz_copy(lay, l).start()

    loop(n_layer, send_plane_grad)
    own = gz_send[l]
    for k in range(n_layer - 1):
        lay = lax.rem(l + 1 + k, n_layer)
        gz_copy(lay, lay).wait_recv()
        own = own + gz_recv[lay]

    @pl.when(kind == 1)
    def _():
        ia_copy().wait_recv()

    def wait_inverse(slot):
        @pl.when(jnp.logical_or(kind == 0, kind * n_half + slot != d))
        def _():
            ig_copy(d, l, slot).wait_recv()

    loop(n_half, wait_inverse)

    def piece(dp, lay):
        return out.at[
            lay // 2,
            pl.ds(pl.multiple_of(dp * block, block), block),
            pl.ds(pl.multiple_of((lay % 2) * half, half), half),
        ]

    left = high(inv_a[...], own)
    for j in range(n_half):
        value = high(left[:, j * block : (j + 1) * block], inv_g[j]).astype(jnp.bfloat16)
        out[
            level,
            pl.ds(pl.multiple_of(d * block, block), block),
            pl.ds(pl.multiple_of(kind * half + j * block, block), block),
        ] = value

    def uz_copy(lay, of):
        return remote(piece(d, of), piece(d, of), s_uz.at[lay], r_u.at[d, of], (d, lay))

    def up_copy(c, lay, of):
        return remote(piece(of, lay), piece(of, lay), s_up.at[c, lay], r_u.at[of, lay], (2 * c + core, l))

    def uc_copy(of, lay):
        return remote(piece(of, lay), piece(of, lay), s_uc.at[of // 2, lay], r_u.at[of, lay], sib)

    def forward(lay):
        loop(n_chip - 1, lambda k: up_copy(other(k), lay, d).start())
        uc_copy(d, lay).start()

    loop(n_layer - 1, lambda k: uz_copy(lax.rem(l + 1 + k, n_layer), l).start())
    forward(l)

    def pass_on(k):
        lay = lax.rem(l + 1 + k, n_layer)
        uz_copy(lay, lay).wait_recv()
        forward(lay)

    loop(n_layer - 1, pass_on)

    def to_sibling(i):
        of = 2 * other(i // n_layer) + core
        lay = lax.rem(l + i % n_layer, n_layer)
        up_copy(other(i // n_layer), lay, of).wait_recv()
        uc_copy(of, lay).start()

    loop((n_chip - 1) * n_layer, to_sibling)
    loop(n_chip * n_layer, lambda i: uc_copy(2 * (i // n_layer) + 1 - core, i % n_layer).wait_recv())

    def sent_chip(c):
        fc_copy(c).wait_send()
        gc_copy(c).wait_send()
        loop(n_layer, lambda lay: uc_copy(2 * c + core, lay).wait_send())

    def sent_plane(k):
        c = other(k)
        fp_copy(c, chip).wait_send()

        def sent(lay):
            gp_copy(c, lay, chip).wait_send()
            up_copy(c, lay, d).wait_send()

        loop(n_layer, sent)

    def sent_layer(k):
        lay = lax.rem(l + 1 + k, n_layer)
        fz_copy(lay, l).wait_send()
        gz_copy(lay, l).wait_send()
        uz_copy(lay, l).wait_send()

    loop(n_chip, sent_chip)
    loop(n_chip - 1, sent_plane)
    loop(n_layer - 1, sent_layer)
    loop(n_dp - 1, lambda k: tr_copy(lax.rem(d + 1 + k, n_dp), d).wait_send())

    @pl.when(kind == 0)
    def _():
        ia_copy().wait_send()

    @pl.when(kind == 1)
    def _():
        loop(n_dp - 1, lambda k: ig_copy(lax.rem(d + 1 + k, n_dp), user, d % n_half).wait_send())

        @pl.when(user != l)
        def _():
            ig_copy(d, user, d % n_half).wait_send()


def exchange(stacks, deltas, n_dp, n_layer, total):
    levels = len(stacks)
    width = stacks[0].shape[1]
    block, half = width // n_dp, width // 2
    n_chip = n_dp // 2
    f32, bf16 = jnp.float32, jnp.bfloat16
    dma = pltpu.SemaphoreType.DMA
    factors, grads = (n_layer, block, block), (n_layer, block, half)
    scratch = [
        pltpu.VMEM((n_chip, *factors), f32),
        pltpu.VMEM((n_chip, *factors), f32),
        pltpu.VMEM((n_chip, *factors), f32),
        pltpu.VMEM((n_chip, *factors), f32),
        pltpu.VMEM(factors, f32),
        pltpu.VMEM(factors, f32),
        pltpu.VMEM((8, 128), f32),
        pltpu.VMEM((n_dp, 8, 128), f32),
        pltpu.VMEM((block, block), f32),
        pltpu.VMEM((block, block), f32),
        pltpu.VMEM((n_dp // 2, block, block), f32),
        pltpu.VMEM((n_chip, *grads), f32),
        pltpu.VMEM((n_chip, *grads), f32),
        pltpu.VMEM((n_chip, *grads), f32),
        pltpu.VMEM((n_chip, *grads), f32),
        pltpu.VMEM(grads, f32),
        pltpu.VMEM(grads, f32),
        dma((n_chip,)), dma((n_chip,)),
        dma((n_chip,)), dma((n_chip,)),
        dma((n_layer,)), dma((n_layer,)),
        dma((n_dp,)), dma((n_dp,)),
        dma, dma,
        dma((n_dp,)), dma((n_dp // 2,)),
        dma((n_chip,)), dma((n_chip,)),
        dma((n_chip, n_layer)), dma((n_chip, n_layer)),
        dma((n_layer,)), dma((n_layer,)),
        dma((n_layer,)), dma((n_chip, n_layer)), dma((n_chip, n_layer)), dma((n_dp, n_layer)),
    ]
    return pl.pallas_call(
        functools.partial(exchange_kernel, n_dp, n_layer, float(total)),
        out_shape=jax.ShapeDtypeStruct((levels, width, width), bf16),
        in_specs=[pl.BlockSpec(memory_space=pltpu.VMEM)] * (2 * levels),
        out_specs=pl.BlockSpec(memory_space=pltpu.VMEM),
        scratch_shapes=scratch,
        compiler_params=pltpu.CompilerParams(
            collective_id=0, has_side_effects=True, vmem_limit_bytes=48 * 2**20
        ),
        name="exchange",
    )(*stacks, *deltas)


def shards(coords, sample_ids, pool, in_weight, in_bias, hidden, out_weight):
    n_dp = lax.axis_size("dp")
    n_layer = lax.axis_size("layer")
    points_here = coords.shape[1]
    total = points_here * n_dp * n_layer
    width = hidden.shape[1]
    levels = hidden.shape[0]
    block = width // n_dp
    half_width = width // 2
    dp_index = lax.axis_index("dp")
    layer_index = lax.axis_index("layer")
    level_own = layer_index // 2
    kind_own = layer_index % 2
    weight = jax.nn.softplus(pool[sample_ids])
    losses, stacks, deltas = point_terms(
        coords, weight, in_weight, in_bias, hidden, out_weight, total
    )
    if block % 128 == 0 and n_layer == 2 * levels:
        return (exchange(stacks, deltas, n_dp, n_layer, total), losses)
    factor_list = []
    grad_list = []
    for level in range(levels):
        rows_a = stacks[level].reshape(-1, n_dp, block)
        rows_g = deltas[level].reshape(-1, n_dp, block)
        part_a = (
            jnp.einsum("rnb,rnc->nbc", rows_a, rows_a, preferred_element_type=jnp.float32) / total
        )
        part_g = (
            jnp.einsum("rnb,rnc->nbc", rows_g, rows_g, preferred_element_type=jnp.float32) * total
        )
        factor_list.append(jnp.stack([part_a, part_g], axis=1))
        halves = deltas[level].reshape(-1, 2, half_width)
        grad_list.append(
            jnp.einsum("rnb,rhc->nhbc", rows_a, halves, preferred_element_type=jnp.float32)
        )
    factor_terms = jnp.stack(factor_list, axis=1).reshape(n_dp * levels * 2, block * block)
    grad_terms = jnp.stack(grad_list, axis=1).reshape(n_dp * levels * 2 * block, half_width)
    owned = lax.psum_scatter(
        factor_terms, ("dp", "layer"), scatter_dimension=0, tiled=True
    ).reshape(block, block)
    own_trace = jnp.trace(owned)
    marked = jnp.where(jnp.arange(n_layer) == layer_index, own_trace, 0.0)
    totals = lax.psum(marked, ("dp", "layer"))
    inverse = damped_inverse(owned, totals[layer_index] / width)
    inverses = lax.all_gather(
        inverse.reshape(1, block * block), ("dp", "layer"), axis=0, tiled=True
    )
    inverses = inverses.reshape(n_dp, levels, 2, block, block)
    inv_a = inverses[dp_index, level_own, 0]
    inv_g_all = inverses[:, level_own, 1]
    inv_g = lax.dynamic_slice_in_dim(inv_g_all, kind_own * (n_dp // 2), n_dp // 2, 0)
    owned_grad = lax.psum_scatter(grad_terms, ("dp", "layer"), scatter_dimension=0, tiled=True)
    left = jnp.dot(inv_a, owned_grad, precision=lax.Precision.HIGHEST).reshape(
        block, n_dp // 2, block
    )
    right = jnp.einsum("ajc,jcq->ajq", left, inv_g, precision=lax.Precision.HIGHEST)
    update_block = right.reshape(1, block, half_width).astype(jnp.bfloat16)
    gathered = lax.all_gather(update_block, ("dp", "layer"), axis=0, tiled=True)
    update = (
        gathered.reshape(n_dp, levels, 2, block, half_width)
        .transpose(1, 0, 3, 2, 4)
        .reshape(levels, width, width)
    )
    return (update, losses)


def solution(mesh):
    return jax.shard_map(
        shards,
        mesh=mesh,
        in_specs=(P(None, ("dp", "layer")), P(("dp", "layer")), P("dp"), P(), P(), P(), P()),
        out_specs=(P(), P(("dp", "layer"))),
        check_vma=False,
    )
```

```python
import functools

import jax
import jax.numpy as jnp
from jax import lax
from jax.experimental import pallas as pl
from jax.experimental.pallas import tpu as pltpu
from jax.sharding import PartitionSpec as P

VISCOSITY = 0.1
DAMPING = 0.1


def taylor_tanh(pre, pre_grad, pre_lap):
    act = jnp.tanh(pre)
    slope = 1.0 - act * act
    act_lap = slope * pre_lap - 2.0 * act * slope * jnp.sum(pre_grad * pre_grad, axis=0)
    return (act, slope * pre_grad, act_lap)


def network(nudges, coords, in_weight, in_bias, hidden, out_weight):
    count = coords.shape[1]
    width = in_weight.shape[1]
    pre = jnp.dot(coords.T, in_weight, precision=lax.Precision.HIGHEST) + in_bias
    pre_grad = jnp.broadcast_to(in_weight[:, None, :], (3, count, width))
    pre_lap = jnp.zeros((count, width), in_weight.dtype)
    stacks = []
    for level in range(hidden.shape[0]):
        act, act_grad, act_lap = taylor_tanh(pre, pre_grad, pre_lap)
        stack = (
            jnp.concatenate([act[None], act_grad, act_lap[None]], 0)
            .astype(jnp.bfloat16)
            .reshape(5 * count, width)
        )
        stacks.append(stack)
        mixed = jnp.dot(stack, hidden[level], preferred_element_type=jnp.float32) + nudges[level]
        mixed = mixed.reshape(5, count, width)
        pre, pre_grad, pre_lap = (mixed[0], mixed[1:4], mixed[4])
    act, act_grad, act_lap = taylor_tanh(pre, pre_grad, pre_lap)
    field = jnp.dot(act, out_weight, precision=lax.Precision.HIGHEST)
    field_grad = jnp.einsum("kpw,wc->kpc", act_grad, out_weight, precision=lax.Precision.HIGHEST)
    field_lap = jnp.dot(act_lap, out_weight, precision=lax.Precision.HIGHEST)
    return (field, field_grad, field_lap, stacks)


def residual_loss(field, field_grad, field_lap):
    velocity = field[:, :3].T
    advect = jnp.sum(velocity[:, :, None] * field_grad[:, :, :3], axis=0)
    momentum = advect + field_grad[:, :, 3].T - VISCOSITY * field_lap[:, :3]
    continuity = field_grad[0, :, 0] + field_grad[1, :, 1] + field_grad[2, :, 2]
    return 0.5 * (jnp.sum(momentum * momentum, axis=1) + continuity * continuity)


def point_terms(coords, weight, in_weight, in_bias, hidden, out_weight, total):
    count = coords.shape[1]
    width = in_weight.shape[1]
    zeros = [jnp.zeros((5 * count, width), jnp.float32) for level in range(hidden.shape[0])]

    def loss_of(nudges):
        field, field_grad, field_lap, stacks = network(
            nudges, coords, in_weight, in_bias, hidden, out_weight
        )
        losses = residual_loss(field, field_grad, field_lap)
        return (jnp.sum(weight * losses) / total, (losses, stacks))

    value, pull, extra = jax.vjp(loss_of, zeros, has_aux=True)
    losses, stacks = extra
    deltas = [piece.astype(jnp.bfloat16) for piece in pull(jnp.ones_like(value))[0]]
    return (losses, stacks, deltas)


def damped_inverse(factor, scale):
    size = factor.shape[-1]
    eye = jnp.eye(size, dtype=jnp.float32)
    damped = factor + DAMPING * scale * eye
    lower = jnp.linalg.cholesky(damped)
    return jax.scipy.linalg.cho_solve((lower, True), jnp.broadcast_to(eye, damped.shape))


MESH = pl.DeviceIdType.MESH
TN = (((0,), (0,)), ((), ()))


def mm(a, b, dims):
    return lax.dot_general(a, b, dims, preferred_element_type=jnp.float32)


def high(a, b):
    return jnp.dot(a, b, precision=lax.Precision.HIGHEST, preferred_element_type=jnp.float32)


def eliminate(damped, first, last):
    size = damped.shape[0]
    row_id = lax.broadcasted_iota(jnp.int32, (size, size), 0)
    col_id = lax.broadcasted_iota(jnp.int32, (size, size), 1)

    def step(k, a):
        in_row = row_id == k
        in_col = col_id == k
        row = jnp.sum(jnp.where(in_row, a, 0.0), axis=0, keepdims=True)
        col = jnp.sum(jnp.where(in_col, a, 0.0), axis=1, keepdims=True)
        pivot = jnp.sum(jnp.where(in_col[:1], row, 0.0), axis=1, keepdims=True)
        row = jnp.where(in_col[:1], 1.0, row) * (1.0 / pivot)
        col = jnp.where(in_row[:, :1], -1.0, col)
        return jnp.where(in_row | in_col, 0.0, a) - col * row

    return lax.fori_loop(first, last, step, damped)


def exchange_kernel(
    n_dp, n_layer, total, *refs
):
    levels = n_layer // 2
    n_chip = n_dp // 2
    stacks, deltas = refs[:levels], refs[levels : 2 * levels]
    (out, f_send, f_own, fc_recv, fp_recv, fz_send, fz_recv, tr_send, tr_recv, inv_own, inv_a, inv_g,
     g_send, g_own, gc_recv, gp_recv, gz_send, gz_recv,
     s_fc, r_fc, s_fp, r_fp, s_fz, r_fz, s_tr, r_tr, s_ia, r_ia, s_ig, r_ig,
     s_gc, r_gc, s_gp, r_gp, s_gz, r_gz, s_uz, s_up, s_uc, r_u, s_ga, r_ga, s_uf) = refs[2 * levels :]
    width = stacks[0].shape[1]
    block = width // n_dp
    half = width // 2
    n_half = n_dp // 2
    d = lax.axis_index("dp")
    l = lax.axis_index("layer")
    chip, core = d // 2, d % 2
    level, kind = l // 2, l % 2
    sib = (chip * 2 + 1 - core, l)
    near_x = chip + 1 - 2 * (chip % 2)
    near_y = lax.rem(chip + 2, n_chip)
    across = n_chip - 1 - chip
    quarter = half // 2

    def remote(src, dst, send, recv, dev):
        return pltpu.make_async_remote_copy(
            src_ref=src, dst_ref=dst, send_sem=send, recv_sem=recv, device_id=dev, device_id_type=MESH
        )

    def other(k):
        return lax.rem(chip + 1 + k, n_chip)

    def loop(n, body):
        def run(i, carry):
            body(i)
            return carry

        lax.fori_loop(0, n, run, 0)

    barrier = pltpu.get_barrier_semaphore()

    def greet(k):
        to = lax.rem(d + 1 + k, n_dp)
        pl.semaphore_signal(barrier, inc=1, device_id=(to, l), device_id_type=MESH)

    def greet_mate(k):
        pl.semaphore_signal(barrier, inc=1, device_id=(k, 2 * level + 1 - kind), device_id_type=MESH)

    def greet_layer(k):
        to = lax.rem(2 * level + 2 + k, n_layer)
        pl.semaphore_signal(barrier, inc=1, device_id=(d, to), device_id_type=MESH)

    loop(n_dp - 1, greet)
    loop(n_dp, greet_mate)
    loop(n_layer - 2, greet_layer)

    def columns(ref, dp):
        return ref[:, pl.ds(pl.multiple_of(dp * block, block), block)]

    def factor(lay, dp):
        rows = columns(stacks[lay // 2] if lay % 2 == 0 else deltas[lay // 2], dp)
        term = mm(rows, rows, TN)
        return term / total if lay % 2 == 0 else term * total

    def grad(lay, dp):
        cols = slice((lay % 2) * half, (lay % 2 + 1) * half)
        return mm(columns(stacks[lay // 2], dp), deltas[lay // 2][:, cols], TN)

    def fc_copy(c):
        return remote(f_send.at[c], fc_recv.at[c], s_fc.at[c], r_fc.at[c], sib)

    def gc_copy(c):
        return remote(g_send.at[c], gc_recv.at[c], s_gc.at[c], r_gc.at[c], sib)

    def fp_copy(c, slot):
        return remote(f_own.at[c], fp_recv.at[slot], s_fp.at[c], r_fp.at[slot], (2 * c + core, l))

    def gp_copy(c, lay, slot):
        return remote(
            g_own.at[c, lay], gp_recv.at[slot, lay], s_gp.at[c, lay], r_gp.at[slot, lay], (2 * c + core, l)
        )

    def fz_copy(lay, slot):
        return remote(fz_send.at[lay], fz_recv.at[slot], s_fz.at[lay], r_fz.at[slot], (d, lay))

    def gz_copy(lay, slot):
        return remote(gz_send.at[lay], gz_recv.at[slot], s_gz.at[lay], r_gz.at[slot], (d, lay))

    def first_factor(k):
        c = other(k)
        for lay in range(n_layer):
            f_send[c, lay] = factor(lay, 2 * c + 1 - core)

    loop(n_chip, first_factor)
    pl.semaphore_wait(barrier, 2 * n_dp - 1 + n_layer - 2)
    loop(n_chip, lambda k: fc_copy(other(k)).start())

    def first_grad(k):
        c = other(k)
        for lay in range(n_layer):
            g_send[c, lay] = grad(lay, 2 * c + 1 - core)
        gc_copy(c).start()

    loop(n_chip, first_grad)

    def second_factor(k):
        c = other(k)
        fc_copy(c).wait_recv()
        for lay in range(n_layer):
            f_own[c, lay] = factor(lay, 2 * c + core) + fc_recv[c, lay]

    def send_factor(k):
        second_factor(k)
        fp_copy(other(k), chip).start()

    loop(n_chip - 1, send_factor)
    second_factor(n_chip - 1)

    def second_grad(k):
        c = other(k)
        gc_copy(c).wait_recv()
        for lay in range(n_layer):
            g_own[c, lay] = grad(lay, 2 * c + core) + gc_recv[c, lay]

    loop(n_chip, second_grad)

    def turn(k):
        return lax.rem(l + 1 + k, n_layer)

    def ga_copy(way, lay):
        to, slot = ((near_x, near_y), (near_y, near_x))[way]
        cols = pl.ds(way * quarter, quarter)
        return remote(
            g_own.at[across, lay, :, cols], gp_recv.at[slot, lay, :, cols],
            s_ga.at[way, lay], r_ga.at[way, lay], (2 * to + core, l),
        )

    def start_across(k):
        ga_copy(0, turn(k)).start()
        ga_copy(1, turn(k)).start()

    loop(n_layer, start_across)

    def arrived_across(way, lay):
        cols = pl.ds(way * quarter, quarter)
        return remote(
            g_own.at[across, lay, :, cols], gp_recv.at[across, lay, :, cols],
            s_ga.at[way, lay], r_ga.at[way, lay], (2 * near_x + core, l),
        )

    def relay(k):
        lay = turn(k)
        for way, to in ((0, near_y), (1, near_x)):
            cols = slice(way * quarter, (way + 1) * quarter)
            arrived_across(way, lay).wait_recv()
            g_own[to, lay, :, cols] = g_own[to, lay, :, cols] + gp_recv[across, lay, :, cols]
            gp_copy(to, lay, chip).start()

    loop(n_chip - 1, lambda k: fp_copy(other(k), other(k)).wait_recv())

    def plane_factor(lay):
        value = f_own[chip, lay]
        for k in range(n_chip - 1):
            value = value + fp_recv[other(k), lay]
        fz_send[lay] = value

    def send_plane_factor(k):
        lay = lax.rem(l + 1 + k, n_layer)
        plane_factor(lay)
        fz_copy(lay, l).start()

    loop(n_layer - 1, send_plane_factor)
    plane_factor(l)
    loop(n_layer // 2, relay)
    mine = fz_send[l]
    for k in range(n_layer - 1):
        lay = lax.rem(l + 1 + k, n_layer)
        fz_copy(lay, lay).wait_recv()
        mine = mine + fz_recv[lay]

    diagonal = lax.broadcasted_iota(jnp.int32, (block, block), 0) == lax.broadcasted_iota(
        jnp.int32, (block, block), 1
    )
    trace = jnp.sum(jnp.sum(jnp.where(diagonal, mine, 0.0), axis=0, keepdims=True), axis=1, keepdims=True)
    tr_send[...] = jnp.broadcast_to(trace, tr_send.shape)

    def tr_copy(to, slot):
        return remote(tr_send, tr_recv.at[slot], s_tr.at[to], r_tr.at[slot], (to, l))

    loop(n_dp - 1, lambda k: tr_copy(lax.rem(d + 1 + k, n_dp), d).start())
    loop(n_layer - n_layer // 2, lambda k: relay(n_layer // 2 + k))
    traces = tr_send[...]
    for k in range(n_dp - 1):
        to = lax.rem(d + 1 + k, n_dp)
        tr_copy(to, to).wait_recv()
        traces = traces + tr_recv[to]
    damped = mine + jnp.where(diagonal, DAMPING / width * traces[:1], 0.0)

    def plane_grad(lay):
        value = g_own[chip, lay]
        for c in (near_x, near_y):
            gp_copy(c, lay, c).wait_recv()
            value = value + gp_recv[c, lay]
        gz_send[lay] = value

    def send_plane_grad(k):
        plane_grad(turn(k))
        gz_copy(turn(k), l).start()

    early = n_layer // 2
    part = block // (early + 1)
    for k in range(early):
        damped = eliminate(damped, k * part, (k + 1) * part)
        send_plane_grad(k)
    inv_own[...] = eliminate(damped, early * part, block)

    def ia_copy():
        return remote(inv_own, inv_a, s_ia, r_ia, (d, 2 * level + 1))

    def ig_copy(to, lay, slot):
        return remote(inv_own, inv_g.at[slot], s_ig.at[to], r_ig.at[slot], (to, lay))

    user = 2 * level + d // n_half

    @pl.when(kind == 0)
    def _():
        ia_copy().start()
        inv_a[...] = inv_own[...]

    @pl.when(kind == 1)
    def _():
        loop(n_dp - 1, lambda k: ig_copy(lax.rem(d + 1 + k, n_dp), user, d % n_half).start())

        @pl.when(user == l)
        def _():
            inv_g[d % n_half] = inv_own[...]

        @pl.when(user != l)
        def _():
            ig_copy(d, user, d % n_half).start()

    for k in range(early, n_layer - 1):
        send_plane_grad(k)
    plane_grad(l)
    own = gz_send[l]
    for k in range(n_layer - 1):
        lay = lax.rem(l + 1 + k, n_layer)
        gz_copy(lay, lay).wait_recv()
        own = own + gz_recv[lay]

    @pl.when(kind == 1)
    def _():
        ia_copy().wait_recv()

    def wait_inverse(slot):
        @pl.when(jnp.logical_or(kind == 0, kind * n_half + slot != d))
        def _():
            ig_copy(d, l, slot).wait_recv()

    loop(n_half, wait_inverse)

    def piece(dp, lay):
        return out.at[
            lay // 2,
            pl.ds(pl.multiple_of(dp * block, block), block),
            pl.ds(pl.multiple_of((lay % 2) * half, half), half),
        ]

    left = high(inv_a[...], own)
    for j in range(n_half):
        value = high(left[:, j * block : (j + 1) * block], inv_g[j]).astype(jnp.bfloat16)
        out[
            level,
            pl.ds(pl.multiple_of(d * block, block), block),
            pl.ds(pl.multiple_of(kind * half + j * block, block), block),
        ] = value

    def uz_copy(lay, of):
        return remote(piece(d, of), piece(d, of), s_uz.at[lay], r_u.at[d, of], (d, lay))

    def up_copy(c, lay, of):
        return remote(piece(of, lay), piece(of, lay), s_up.at[c, lay], r_u.at[of, lay], (2 * c + core, l))

    def uc_copy(of, lay):
        return remote(piece(of, lay), piece(of, lay), s_uc.at[of // 2, lay], r_u.at[of, lay], sib)

    def forward(lay):
        up_copy(near_x, lay, d).start()
        up_copy(near_y, lay, d).start()
        uc_copy(d, lay).start()

    loop(n_layer - 1, lambda k: uz_copy(lax.rem(l + 1 + k, n_layer), l).start())
    forward(l)

    def pass_on(k):
        lay = lax.rem(l + 1 + k, n_layer)
        uz_copy(lay, lay).wait_recv()
        forward(lay)

    loop(n_layer - 1, pass_on)

    def uf_copy(to, of, lay):
        return remote(piece(of, lay), piece(of, lay), s_uf.at[lay], r_u.at[of, lay], (2 * to + core, l))

    def from_near(k):
        lay = lax.rem(l + k, n_layer)
        of_x, of_y = 2 * near_x + core, 2 * near_y + core
        up_copy(near_x, lay, of_x).wait_recv()

        @pl.when(lay % 2 == 0)
        def _():
            uf_copy(near_y, of_x, lay).start()

        uc_copy(of_x, lay).start()
        up_copy(near_y, lay, of_y).wait_recv()

        @pl.when(lay % 2 == 1)
        def _():
            uf_copy(near_x, of_y, lay).start()

        uc_copy(of_y, lay).start()

    loop(n_layer, from_near)

    def from_across(k):
        lay = lax.rem(l + k, n_layer)
        of = 2 * across + core
        uf_copy(near_x, of, lay).wait_recv()
        uc_copy(of, lay).start()

    loop(n_layer, from_across)
    loop(n_chip * n_layer, lambda i: uc_copy(2 * (i // n_layer) + 1 - core, i % n_layer).wait_recv())

    def sent_chip(c):
        fc_copy(c).wait_send()
        gc_copy(c).wait_send()
        loop(n_layer, lambda lay: uc_copy(2 * c + core, lay).wait_send())

    def sent_plane(k):
        c = other(k)
        fp_copy(c, chip).wait_send()

    def sent_near(lay):
        for way, c in ((0, near_x), (1, near_y)):
            ga_copy(way, lay).wait_send()
            gp_copy(c, lay, chip).wait_send()
            up_copy(c, lay, d).wait_send()
        uf_copy(near_x, d, lay).wait_send()

    def sent_layer(k):
        lay = lax.rem(l + 1 + k, n_layer)
        fz_copy(lay, l).wait_send()
        gz_copy(lay, l).wait_send()
        uz_copy(lay, l).wait_send()

    loop(n_chip, sent_chip)
    loop(n_chip - 1, sent_plane)
    loop(n_layer, sent_near)
    loop(n_layer - 1, sent_layer)
    loop(n_dp - 1, lambda k: tr_copy(lax.rem(d + 1 + k, n_dp), d).wait_send())

    @pl.when(kind == 0)
    def _():
        ia_copy().wait_send()

    @pl.when(kind == 1)
    def _():
        loop(n_dp - 1, lambda k: ig_copy(lax.rem(d + 1 + k, n_dp), user, d % n_half).wait_send())

        @pl.when(user != l)
        def _():
            ig_copy(d, user, d % n_half).wait_send()


def exchange(stacks, deltas, n_dp, n_layer, total):
    levels = len(stacks)
    width = stacks[0].shape[1]
    block, half = width // n_dp, width // 2
    n_chip = n_dp // 2
    f32, bf16 = jnp.float32, jnp.bfloat16
    dma = pltpu.SemaphoreType.DMA
    factors, grads = (n_layer, block, block), (n_layer, block, half)
    scratch = [
        pltpu.VMEM((n_chip, *factors), f32),
        pltpu.VMEM((n_chip, *factors), f32),
        pltpu.VMEM((n_chip, *factors), f32),
        pltpu.VMEM((n_chip, *factors), f32),
        pltpu.VMEM(factors, f32),
        pltpu.VMEM(factors, f32),
        pltpu.VMEM((8, 128), f32),
        pltpu.VMEM((n_dp, 8, 128), f32),
        pltpu.VMEM((block, block), f32),
        pltpu.VMEM((block, block), f32),
        pltpu.VMEM((n_dp // 2, block, block), f32),
        pltpu.VMEM((n_chip, *grads), f32),
        pltpu.VMEM((n_chip, *grads), f32),
        pltpu.VMEM((n_chip, *grads), f32),
        pltpu.VMEM((n_chip, *grads), f32),
        pltpu.VMEM(grads, f32),
        pltpu.VMEM(grads, f32),
        dma((n_chip,)), dma((n_chip,)),
        dma((n_chip,)), dma((n_chip,)),
        dma((n_layer,)), dma((n_layer,)),
        dma((n_dp,)), dma((n_dp,)),
        dma, dma,
        dma((n_dp,)), dma((n_dp // 2,)),
        dma((n_chip,)), dma((n_chip,)),
        dma((n_chip, n_layer)), dma((n_chip, n_layer)),
        dma((n_layer,)), dma((n_layer,)),
        dma((n_layer,)), dma((n_chip, n_layer)), dma((n_chip, n_layer)), dma((n_dp, n_layer)),
        dma((2, n_layer)), dma((2, n_layer)), dma((n_layer,)),
    ]
    return pl.pallas_call(
        functools.partial(exchange_kernel, n_dp, n_layer, float(total)),
        out_shape=jax.ShapeDtypeStruct((levels, width, width), bf16),
        in_specs=[pl.BlockSpec(memory_space=pltpu.VMEM)] * (2 * levels),
        out_specs=pl.BlockSpec(memory_space=pltpu.VMEM),
        scratch_shapes=scratch,
        compiler_params=pltpu.CompilerParams(
            collective_id=0, has_side_effects=True, vmem_limit_bytes=48 * 2**20
        ),
        name="exchange",
    )(*stacks, *deltas)


def shards(coords, sample_ids, pool, in_weight, in_bias, hidden, out_weight):
    n_dp = lax.axis_size("dp")
    n_layer = lax.axis_size("layer")
    points_here = coords.shape[1]
    total = points_here * n_dp * n_layer
    width = hidden.shape[1]
    levels = hidden.shape[0]
    block = width // n_dp
    half_width = width // 2
    dp_index = lax.axis_index("dp")
    layer_index = lax.axis_index("layer")
    level_own = layer_index // 2
    kind_own = layer_index % 2
    weight = jax.nn.softplus(pool[sample_ids])
    losses, stacks, deltas = point_terms(
        coords, weight, in_weight, in_bias, hidden, out_weight, total
    )
    if block % 128 == 0 and n_dp == 8 and n_layer == 2 * levels:
        return (exchange(stacks, deltas, n_dp, n_layer, total), losses)
    factor_list = []
    grad_list = []
    for level in range(levels):
        rows_a = stacks[level].reshape(-1, n_dp, block)
        rows_g = deltas[level].reshape(-1, n_dp, block)
        part_a = (
            jnp.einsum("rnb,rnc->nbc", rows_a, rows_a, preferred_element_type=jnp.float32) / total
        )
        part_g = (
            jnp.einsum("rnb,rnc->nbc", rows_g, rows_g, preferred_element_type=jnp.float32) * total
        )
        factor_list.append(jnp.stack([part_a, part_g], axis=1))
        halves = deltas[level].reshape(-1, 2, half_width)
        grad_list.append(
            jnp.einsum("rnb,rhc->nhbc", rows_a, halves, preferred_element_type=jnp.float32)
        )
    factor_terms = jnp.stack(factor_list, axis=1).reshape(n_dp * levels * 2, block * block)
    grad_terms = jnp.stack(grad_list, axis=1).reshape(n_dp * levels * 2 * block, half_width)
    owned = lax.psum_scatter(
        factor_terms, ("dp", "layer"), scatter_dimension=0, tiled=True
    ).reshape(block, block)
    own_trace = jnp.trace(owned)
    marked = jnp.where(jnp.arange(n_layer) == layer_index, own_trace, 0.0)
    totals = lax.psum(marked, ("dp", "layer"))
    inverse = damped_inverse(owned, totals[layer_index] / width)
    inverses = lax.all_gather(
        inverse.reshape(1, block * block), ("dp", "layer"), axis=0, tiled=True
    )
    inverses = inverses.reshape(n_dp, levels, 2, block, block)
    inv_a = inverses[dp_index, level_own, 0]
    inv_g_all = inverses[:, level_own, 1]
    inv_g = lax.dynamic_slice_in_dim(inv_g_all, kind_own * (n_dp // 2), n_dp // 2, 0)
    owned_grad = lax.psum_scatter(grad_terms, ("dp", "layer"), scatter_dimension=0, tiled=True)
    left = jnp.dot(inv_a, owned_grad, precision=lax.Precision.HIGHEST).reshape(
        block, n_dp // 2, block
    )
    right = jnp.einsum("ajc,jcq->ajq", left, inv_g, precision=lax.Precision.HIGHEST)
    update_block = right.reshape(1, block, half_width).astype(jnp.bfloat16)
    gathered = lax.all_gather(update_block, ("dp", "layer"), axis=0, tiled=True)
    update = (
        gathered.reshape(n_dp, levels, 2, block, half_width)
        .transpose(1, 0, 3, 2, 4)
        .reshape(levels, width, width)
    )
    return (update, losses)


def solution(mesh):
    return jax.shard_map(
        shards,
        mesh=mesh,
        in_specs=(P(None, ("dp", "layer")), P(("dp", "layer")), P("dp"), P(), P(), P(), P()),
        out_specs=(P(), P(("dp", "layer"))),
        check_vma=False,
    )
```

```python
import functools

import jax
import jax.numpy as jnp
from jax import lax
from jax.experimental import pallas as pl
from jax.experimental.pallas import tpu as pltpu
from jax.sharding import PartitionSpec as P

VISCOSITY = 0.1
DAMPING = 0.1


def taylor_tanh(pre, pre_grad, pre_lap):
    act = jnp.tanh(pre)
    slope = 1.0 - act * act
    act_lap = slope * pre_lap - 2.0 * act * slope * jnp.sum(pre_grad * pre_grad, axis=0)
    return (act, slope * pre_grad, act_lap)


def network(nudges, coords, in_weight, in_bias, hidden, out_weight):
    count = coords.shape[1]
    width = in_weight.shape[1]
    pre = jnp.dot(coords.T, in_weight, precision=lax.Precision.HIGHEST) + in_bias
    pre_grad = jnp.broadcast_to(in_weight[:, None, :], (3, count, width))
    pre_lap = jnp.zeros((count, width), in_weight.dtype)
    stacks = []
    for level in range(hidden.shape[0]):
        act, act_grad, act_lap = taylor_tanh(pre, pre_grad, pre_lap)
        stack = (
            jnp.concatenate([act[None], act_grad, act_lap[None]], 0)
            .astype(jnp.bfloat16)
            .reshape(5 * count, width)
        )
        stacks.append(stack)
        mixed = jnp.dot(stack, hidden[level], preferred_element_type=jnp.float32) + nudges[level]
        mixed = mixed.reshape(5, count, width)
        pre, pre_grad, pre_lap = (mixed[0], mixed[1:4], mixed[4])
    act, act_grad, act_lap = taylor_tanh(pre, pre_grad, pre_lap)
    field = jnp.dot(act, out_weight, precision=lax.Precision.HIGHEST)
    field_grad = jnp.einsum("kpw,wc->kpc", act_grad, out_weight, precision=lax.Precision.HIGHEST)
    field_lap = jnp.dot(act_lap, out_weight, precision=lax.Precision.HIGHEST)
    return (field, field_grad, field_lap, stacks)


def residual_loss(field, field_grad, field_lap):
    velocity = field[:, :3].T
    advect = jnp.sum(velocity[:, :, None] * field_grad[:, :, :3], axis=0)
    momentum = advect + field_grad[:, :, 3].T - VISCOSITY * field_lap[:, :3]
    continuity = field_grad[0, :, 0] + field_grad[1, :, 1] + field_grad[2, :, 2]
    return 0.5 * (jnp.sum(momentum * momentum, axis=1) + continuity * continuity)


def point_terms(coords, weight, in_weight, in_bias, hidden, out_weight, total):
    count = coords.shape[1]
    width = in_weight.shape[1]
    zeros = [jnp.zeros((5 * count, width), jnp.float32) for level in range(hidden.shape[0])]

    def loss_of(nudges):
        field, field_grad, field_lap, stacks = network(
            nudges, coords, in_weight, in_bias, hidden, out_weight
        )
        losses = residual_loss(field, field_grad, field_lap)
        return (jnp.sum(weight * losses) / total, (losses, stacks))

    value, pull, extra = jax.vjp(loss_of, zeros, has_aux=True)
    losses, stacks = extra
    deltas = [piece.astype(jnp.bfloat16) for piece in pull(jnp.ones_like(value))[0]]
    return (losses, stacks, deltas)


def damped_inverse(factor, scale):
    size = factor.shape[-1]
    eye = jnp.eye(size, dtype=jnp.float32)
    damped = factor + DAMPING * scale * eye
    lower = jnp.linalg.cholesky(damped)
    return jax.scipy.linalg.cho_solve((lower, True), jnp.broadcast_to(eye, damped.shape))


MESH = pl.DeviceIdType.MESH
TN = (((0,), (0,)), ((), ()))


def mm(a, b, dims):
    return lax.dot_general(a, b, dims, preferred_element_type=jnp.float32)


def high(a, b):
    return jnp.dot(a, b, precision=lax.Precision.HIGHEST, preferred_element_type=jnp.float32)


def eliminate(damped, first, last):
    size = damped.shape[0]
    row_id = lax.broadcasted_iota(jnp.int32, (size, size), 0)
    col_id = lax.broadcasted_iota(jnp.int32, (size, size), 1)

    def step(k, a):
        in_row = row_id == k
        in_col = col_id == k
        row = jnp.sum(jnp.where(in_row, a, 0.0), axis=0, keepdims=True)
        col = jnp.sum(jnp.where(in_col, a, 0.0), axis=1, keepdims=True)
        pivot = jnp.sum(jnp.where(in_col[:1], row, 0.0), axis=1, keepdims=True)
        row = jnp.where(in_col[:1], 1.0, row) * (1.0 / pivot)
        col = jnp.where(in_row[:, :1], -1.0, col)
        return jnp.where(in_row | in_col, 0.0, a) - col * row

    return lax.fori_loop(first, last, step, damped)


def exchange_kernel(
    n_dp, n_layer, total, *refs
):
    levels = n_layer // 2
    n_chip = n_dp // 2
    stacks, deltas = refs[:levels], refs[levels : 2 * levels]
    (out, f_send, f_own, fc_recv, fp_recv, fz_send, fz_recv, tr_send, tr_recv, inv_own, inv_a, inv_g,
     g_send, g_own, gc_recv, gp_recv, gz_send, gz_recv,
     s_fc, r_fc, s_fp, r_fp, s_fz, r_fz, s_tr, r_tr, s_ia, r_ia, s_ig, r_ig,
     s_gc, r_gc, s_gp, r_gp, s_gz, r_gz, s_uz, s_up, s_uc, r_u, s_ga, r_ga, s_uf) = refs[2 * levels :]
    width = stacks[0].shape[1]
    block = width // n_dp
    half = width // 2
    n_half = n_dp // 2
    d = lax.axis_index("dp")
    l = lax.axis_index("layer")
    chip, core = d // 2, d % 2
    level, kind = l // 2, l % 2
    sib = (chip * 2 + 1 - core, l)
    near_x = chip + 1 - 2 * (chip % 2)
    near_y = lax.rem(chip + 2, n_chip)
    across = n_chip - 1 - chip
    quarter = half // 2

    def remote(src, dst, send, recv, dev):
        return pltpu.make_async_remote_copy(
            src_ref=src, dst_ref=dst, send_sem=send, recv_sem=recv, device_id=dev, device_id_type=MESH
        )

    def other(k):
        return lax.rem(chip + 1 + k, n_chip)

    def loop(n, body):
        def run(i, carry):
            body(i)
            return carry

        lax.fori_loop(0, n, run, 0)

    barrier = pltpu.get_barrier_semaphore()

    def greet(k):
        to = lax.rem(d + 1 + k, n_dp)
        pl.semaphore_signal(barrier, inc=1, device_id=(to, l), device_id_type=MESH)

    def greet_mate(k):
        pl.semaphore_signal(barrier, inc=1, device_id=(k, 2 * level + 1 - kind), device_id_type=MESH)

    def greet_layer(k):
        to = lax.rem(2 * level + 2 + k, n_layer)
        pl.semaphore_signal(barrier, inc=1, device_id=(d, to), device_id_type=MESH)

    loop(n_dp - 1, greet)
    loop(n_dp, greet_mate)
    loop(n_layer - 2, greet_layer)

    def columns(ref, dp):
        return ref[:, pl.ds(pl.multiple_of(dp * block, block), block)]

    def factor(lay, dp):
        rows = columns(stacks[lay // 2] if lay % 2 == 0 else deltas[lay // 2], dp)
        term = mm(rows, rows, TN)
        return term / total if lay % 2 == 0 else term * total

    def grad(lay, dp):
        cols = slice((lay % 2) * half, (lay % 2 + 1) * half)
        return mm(columns(stacks[lay // 2], dp), deltas[lay // 2][:, cols], TN)

    def fc_copy(c):
        return remote(f_send.at[c], fc_recv.at[c], s_fc.at[c], r_fc.at[c], sib)

    def gc_copy(c):
        return remote(g_send.at[c], gc_recv.at[c], s_gc.at[c], r_gc.at[c], sib)

    def fp_copy(c, slot):
        return remote(f_own.at[c], fp_recv.at[slot], s_fp.at[c], r_fp.at[slot], (2 * c + core, l))

    def gp_copy(c, lay, slot):
        return remote(
            g_own.at[c, lay], gp_recv.at[slot, lay], s_gp.at[c, lay], r_gp.at[slot, lay], (2 * c + core, l)
        )

    def fz_copy(lay, slot):
        return remote(fz_send.at[lay], fz_recv.at[slot], s_fz.at[lay], r_fz.at[slot], (d, lay))

    def gz_copy(lay, slot):
        return remote(gz_send.at[lay], gz_recv.at[slot], s_gz.at[lay], r_gz.at[slot], (d, lay))

    def first_factor(k):
        c = other(k)
        for lay in range(n_layer):
            f_send[c, lay] = factor(lay, 2 * c + 1 - core)

    loop(n_chip, first_factor)
    pl.semaphore_wait(barrier, 2 * n_dp - 1 + n_layer - 2)
    loop(n_chip, lambda k: fc_copy(other(k)).start())

    def first_grad(k):
        c = other(k)
        for lay in range(n_layer):
            g_send[c, lay] = grad(lay, 2 * c + 1 - core)
        gc_copy(c).start()

    loop(n_chip, first_grad)

    def second_factor(k):
        c = other(k)
        fc_copy(c).wait_recv()
        for lay in range(n_layer):
            f_own[c, lay] = factor(lay, 2 * c + core) + fc_recv[c, lay]

    def send_factor(k):
        second_factor(k)
        fp_copy(other(k), chip).start()

    loop(n_chip - 1, send_factor)
    second_factor(n_chip - 1)

    def second_grad(k):
        c = other(k)
        gc_copy(c).wait_recv()
        for lay in range(n_layer):
            g_own[c, lay] = grad(lay, 2 * c + core) + gc_recv[c, lay]

    loop(n_chip, second_grad)

    def turn(k):
        return lax.rem(l + 1 + k, n_layer)

    def ga_copy(way, lay):
        to, slot = ((near_x, near_y), (near_y, near_x))[way]
        cols = pl.ds(way * quarter, quarter)
        return remote(
            g_own.at[across, lay, :, cols], gp_recv.at[slot, lay, :, cols],
            s_ga.at[way, lay], r_ga.at[way, lay], (2 * to + core, l),
        )

    def start_across(k):
        ga_copy(0, turn(k)).start()
        ga_copy(1, turn(k)).start()

    loop(n_layer, start_across)

    def arrived_across(way, lay):
        cols = pl.ds(way * quarter, quarter)
        return remote(
            g_own.at[across, lay, :, cols], gp_recv.at[across, lay, :, cols],
            s_ga.at[way, lay], r_ga.at[way, lay], (2 * near_x + core, l),
        )

    def relay(k):
        lay = turn(k)
        for way, to in ((0, near_y), (1, near_x)):
            cols = slice(way * quarter, (way + 1) * quarter)
            arrived_across(way, lay).wait_recv()
            g_own[to, lay, :, cols] = g_own[to, lay, :, cols] + gp_recv[across, lay, :, cols]
            gp_copy(to, lay, chip).start()

    loop(n_chip - 1, lambda k: fp_copy(other(k), other(k)).wait_recv())

    def plane_factor(lay):
        value = f_own[chip, lay]
        for k in range(n_chip - 1):
            value = value + fp_recv[other(k), lay]
        fz_send[lay] = value

    def send_plane_factor(k):
        lay = lax.rem(l + 1 + k, n_layer)
        plane_factor(lay)
        fz_copy(lay, l).start()

    loop(n_layer - 1, send_plane_factor)
    plane_factor(l)
    loop(n_layer // 2, relay)
    mine = fz_send[l]
    for k in range(n_layer - 1):
        lay = lax.rem(l + 1 + k, n_layer)
        fz_copy(lay, lay).wait_recv()
        mine = mine + fz_recv[lay]

    diagonal = lax.broadcasted_iota(jnp.int32, (block, block), 0) == lax.broadcasted_iota(
        jnp.int32, (block, block), 1
    )
    trace = jnp.sum(jnp.sum(jnp.where(diagonal, mine, 0.0), axis=0, keepdims=True), axis=1, keepdims=True)
    tr_send[...] = jnp.broadcast_to(trace, tr_send.shape)

    def tr_copy(to, slot):
        return remote(tr_send, tr_recv.at[slot], s_tr.at[to], r_tr.at[slot], (to, l))

    loop(n_dp - 1, lambda k: tr_copy(lax.rem(d + 1 + k, n_dp), d).start())
    loop(n_layer - n_layer // 2, lambda k: relay(n_layer // 2 + k))
    traces = tr_send[...]
    for k in range(n_dp - 1):
        to = lax.rem(d + 1 + k, n_dp)
        tr_copy(to, to).wait_recv()
        traces = traces + tr_recv[to]
    damped = mine + jnp.where(diagonal, DAMPING / width * traces[:1], 0.0)

    def plane_grad(lay):
        value = g_own[chip, lay]
        for c in (near_x, near_y):
            gp_copy(c, lay, c).wait_recv()
            value = value + gp_recv[c, lay]
        gz_send[lay] = value

    def send_plane_grad(k):
        plane_grad(turn(k))
        gz_copy(turn(k), l).start()

    early = n_layer - 1
    part = block // (early + 1)
    for k in range(early):
        send_plane_grad(k)
        damped = eliminate(damped, k * part, (k + 1) * part)
    inv_own[...] = eliminate(damped, early * part, block)

    def ia_copy():
        return remote(inv_own, inv_a, s_ia, r_ia, (d, 2 * level + 1))

    def ig_copy(to, lay, slot):
        return remote(inv_own, inv_g.at[slot], s_ig.at[to], r_ig.at[slot], (to, lay))

    user = 2 * level + d // n_half

    @pl.when(kind == 0)
    def _():
        ia_copy().start()
        inv_a[...] = inv_own[...]

    @pl.when(kind == 1)
    def _():
        loop(n_dp - 1, lambda k: ig_copy(lax.rem(d + 1 + k, n_dp), user, d % n_half).start())

        @pl.when(user == l)
        def _():
            inv_g[d % n_half] = inv_own[...]

        @pl.when(user != l)
        def _():
            ig_copy(d, user, d % n_half).start()

    for k in range(early, n_layer - 1):
        send_plane_grad(k)
    plane_grad(l)
    own = gz_send[l]
    for k in range(n_layer - 1):
        lay = lax.rem(l + 1 + k, n_layer)
        gz_copy(lay, lay).wait_recv()
        own = own + gz_recv[lay]

    @pl.when(kind == 1)
    def _():
        ia_copy().wait_recv()

    def wait_inverse(slot):
        @pl.when(jnp.logical_or(kind == 0, kind * n_half + slot != d))
        def _():
            ig_copy(d, l, slot).wait_recv()

    loop(n_half, wait_inverse)

    def piece(dp, lay):
        return out.at[
            lay // 2,
            pl.ds(pl.multiple_of(dp * block, block), block),
            pl.ds(pl.multiple_of((lay % 2) * half, half), half),
        ]

    left = high(inv_a[...], own)
    for j in range(n_half):
        value = high(left[:, j * block : (j + 1) * block], inv_g[j]).astype(jnp.bfloat16)
        out[
            level,
            pl.ds(pl.multiple_of(d * block, block), block),
            pl.ds(pl.multiple_of(kind * half + j * block, block), block),
        ] = value

    def uz_copy(lay, of):
        return remote(piece(d, of), piece(d, of), s_uz.at[lay], r_u.at[d, of], (d, lay))

    def up_copy(c, lay, of):
        return remote(piece(of, lay), piece(of, lay), s_up.at[c, lay], r_u.at[of, lay], (2 * c + core, l))

    def uc_copy(of, lay):
        return remote(piece(of, lay), piece(of, lay), s_uc.at[of // 2, lay], r_u.at[of, lay], sib)

    def forward(lay):
        up_copy(near_x, lay, d).start()
        up_copy(near_y, lay, d).start()
        uc_copy(d, lay).start()

    loop(n_layer - 1, lambda k: uz_copy(lax.rem(l + 1 + k, n_layer), l).start())
    forward(l)

    def pass_on(k):
        lay = lax.rem(l + 1 + k, n_layer)
        uz_copy(lay, lay).wait_recv()
        forward(lay)

    loop(n_layer - 1, pass_on)

    def uf_copy(to, of, lay):
        return remote(piece(of, lay), piece(of, lay), s_uf.at[lay], r_u.at[of, lay], (2 * to + core, l))

    def from_near(k):
        lay = lax.rem(l + k, n_layer)
        of_x, of_y = 2 * near_x + core, 2 * near_y + core
        up_copy(near_x, lay, of_x).wait_recv()

        @pl.when(lay % 2 == 0)
        def _():
            uf_copy(near_y, of_x, lay).start()

        uc_copy(of_x, lay).start()
        up_copy(near_y, lay, of_y).wait_recv()

        @pl.when(lay % 2 == 1)
        def _():
            uf_copy(near_x, of_y, lay).start()

        uc_copy(of_y, lay).start()

    loop(n_layer, from_near)

    def from_across(k):
        lay = lax.rem(l + k, n_layer)
        of = 2 * across + core
        uf_copy(near_x, of, lay).wait_recv()
        uc_copy(of, lay).start()

    loop(n_layer, from_across)
    loop(n_chip * n_layer, lambda i: uc_copy(2 * (i // n_layer) + 1 - core, i % n_layer).wait_recv())

    def sent_chip(c):
        fc_copy(c).wait_send()
        gc_copy(c).wait_send()
        loop(n_layer, lambda lay: uc_copy(2 * c + core, lay).wait_send())

    def sent_plane(k):
        c = other(k)
        fp_copy(c, chip).wait_send()

    def sent_near(lay):
        for way, c in ((0, near_x), (1, near_y)):
            ga_copy(way, lay).wait_send()
            gp_copy(c, lay, chip).wait_send()
            up_copy(c, lay, d).wait_send()
        uf_copy(near_x, d, lay).wait_send()

    def sent_layer(k):
        lay = lax.rem(l + 1 + k, n_layer)
        fz_copy(lay, l).wait_send()
        gz_copy(lay, l).wait_send()
        uz_copy(lay, l).wait_send()

    loop(n_chip, sent_chip)
    loop(n_chip - 1, sent_plane)
    loop(n_layer, sent_near)
    loop(n_layer - 1, sent_layer)
    loop(n_dp - 1, lambda k: tr_copy(lax.rem(d + 1 + k, n_dp), d).wait_send())

    @pl.when(kind == 0)
    def _():
        ia_copy().wait_send()

    @pl.when(kind == 1)
    def _():
        loop(n_dp - 1, lambda k: ig_copy(lax.rem(d + 1 + k, n_dp), user, d % n_half).wait_send())

        @pl.when(user != l)
        def _():
            ig_copy(d, user, d % n_half).wait_send()


def exchange(stacks, deltas, n_dp, n_layer, total):
    levels = len(stacks)
    width = stacks[0].shape[1]
    block, half = width // n_dp, width // 2
    n_chip = n_dp // 2
    f32, bf16 = jnp.float32, jnp.bfloat16
    dma = pltpu.SemaphoreType.DMA
    factors, grads = (n_layer, block, block), (n_layer, block, half)
    scratch = [
        pltpu.VMEM((n_chip, *factors), f32),
        pltpu.VMEM((n_chip, *factors), f32),
        pltpu.VMEM((n_chip, *factors), f32),
        pltpu.VMEM((n_chip, *factors), f32),
        pltpu.VMEM(factors, f32),
        pltpu.VMEM(factors, f32),
        pltpu.VMEM((8, 128), f32),
        pltpu.VMEM((n_dp, 8, 128), f32),
        pltpu.VMEM((block, block), f32),
        pltpu.VMEM((block, block), f32),
        pltpu.VMEM((n_dp // 2, block, block), f32),
        pltpu.VMEM((n_chip, *grads), f32),
        pltpu.VMEM((n_chip, *grads), f32),
        pltpu.VMEM((n_chip, *grads), f32),
        pltpu.VMEM((n_chip, *grads), f32),
        pltpu.VMEM(grads, f32),
        pltpu.VMEM(grads, f32),
        dma((n_chip,)), dma((n_chip,)),
        dma((n_chip,)), dma((n_chip,)),
        dma((n_layer,)), dma((n_layer,)),
        dma((n_dp,)), dma((n_dp,)),
        dma, dma,
        dma((n_dp,)), dma((n_dp // 2,)),
        dma((n_chip,)), dma((n_chip,)),
        dma((n_chip, n_layer)), dma((n_chip, n_layer)),
        dma((n_layer,)), dma((n_layer,)),
        dma((n_layer,)), dma((n_chip, n_layer)), dma((n_chip, n_layer)), dma((n_dp, n_layer)),
        dma((2, n_layer)), dma((2, n_layer)), dma((n_layer,)),
    ]
    return pl.pallas_call(
        functools.partial(exchange_kernel, n_dp, n_layer, float(total)),
        out_shape=jax.ShapeDtypeStruct((levels, width, width), bf16),
        in_specs=[pl.BlockSpec(memory_space=pltpu.VMEM)] * (2 * levels),
        out_specs=pl.BlockSpec(memory_space=pltpu.VMEM),
        scratch_shapes=scratch,
        compiler_params=pltpu.CompilerParams(
            collective_id=0, has_side_effects=True, vmem_limit_bytes=48 * 2**20
        ),
        name="exchange",
    )(*stacks, *deltas)


def shards(coords, sample_ids, pool, in_weight, in_bias, hidden, out_weight):
    n_dp = lax.axis_size("dp")
    n_layer = lax.axis_size("layer")
    points_here = coords.shape[1]
    total = points_here * n_dp * n_layer
    width = hidden.shape[1]
    levels = hidden.shape[0]
    block = width // n_dp
    half_width = width // 2
    dp_index = lax.axis_index("dp")
    layer_index = lax.axis_index("layer")
    level_own = layer_index // 2
    kind_own = layer_index % 2
    weight = jax.nn.softplus(pool[sample_ids])
    losses, stacks, deltas = point_terms(
        coords, weight, in_weight, in_bias, hidden, out_weight, total
    )
    if block % 128 == 0 and n_dp == 8 and n_layer == 2 * levels:
        return (exchange(stacks, deltas, n_dp, n_layer, total), losses)
    factor_list = []
    grad_list = []
    for level in range(levels):
        rows_a = stacks[level].reshape(-1, n_dp, block)
        rows_g = deltas[level].reshape(-1, n_dp, block)
        part_a = (
            jnp.einsum("rnb,rnc->nbc", rows_a, rows_a, preferred_element_type=jnp.float32) / total
        )
        part_g = (
            jnp.einsum("rnb,rnc->nbc", rows_g, rows_g, preferred_element_type=jnp.float32) * total
        )
        factor_list.append(jnp.stack([part_a, part_g], axis=1))
        halves = deltas[level].reshape(-1, 2, half_width)
        grad_list.append(
            jnp.einsum("rnb,rhc->nhbc", rows_a, halves, preferred_element_type=jnp.float32)
        )
    factor_terms = jnp.stack(factor_list, axis=1).reshape(n_dp * levels * 2, block * block)
    grad_terms = jnp.stack(grad_list, axis=1).reshape(n_dp * levels * 2 * block, half_width)
    owned = lax.psum_scatter(
        factor_terms, ("dp", "layer"), scatter_dimension=0, tiled=True
    ).reshape(block, block)
    own_trace = jnp.trace(owned)
    marked = jnp.where(jnp.arange(n_layer) == layer_index, own_trace, 0.0)
    totals = lax.psum(marked, ("dp", "layer"))
    inverse = damped_inverse(owned, totals[layer_index] / width)
    inverses = lax.all_gather(
        inverse.reshape(1, block * block), ("dp", "layer"), axis=0, tiled=True
    )
    inverses = inverses.reshape(n_dp, levels, 2, block, block)
    inv_a = inverses[dp_index, level_own, 0]
    inv_g_all = inverses[:, level_own, 1]
    inv_g = lax.dynamic_slice_in_dim(inv_g_all, kind_own * (n_dp // 2), n_dp // 2, 0)
    owned_grad = lax.psum_scatter(grad_terms, ("dp", "layer"), scatter_dimension=0, tiled=True)
    left = jnp.dot(inv_a, owned_grad, precision=lax.Precision.HIGHEST).reshape(
        block, n_dp // 2, block
    )
    right = jnp.einsum("ajc,jcq->ajq", left, inv_g, precision=lax.Precision.HIGHEST)
    update_block = right.reshape(1, block, half_width).astype(jnp.bfloat16)
    gathered = lax.all_gather(update_block, ("dp", "layer"), axis=0, tiled=True)
    update = (
        gathered.reshape(n_dp, levels, 2, block, half_width)
        .transpose(1, 0, 3, 2, 4)
        .reshape(levels, width, width)
    )
    return (update, losses)


def solution(mesh):
    return jax.shard_map(
        shards,
        mesh=mesh,
        in_specs=(P(None, ("dp", "layer")), P(("dp", "layer")), P("dp"), P(), P(), P(), P()),
        out_specs=(P(), P(("dp", "layer"))),
        check_vma=False,
    )
```
